512 devices in a mesh: row: 32 (over z, x_hi, core), col: 16 (over x_lo, y).
Axes of the slice: x: 4 (x_hi: 2, x_lo: 2; x = x_hi * 2 + x_lo), y: 8, z: 8, core: 2. Of those that a mesh axis runs over, the one named last changes fastest.
Arguments:
- fock_matrix: bfloat16 [12288, 12288], P('row', 'col'), may hold values from -40 to 40, as said below
- density_matrix: bfloat16 [12288, 12288], P('row', 'col'), may hold values from -1.25 to 1.25, as said below
- fock_blocks: int32 [96, 96], replicated, may hold values from 0 to 1, as said below
- density_blocks: int32 [96, 96], replicated, may hold values from 0 to 1, as said below
- slab_offset: int32 [1], replicated, may hold values from 0 to 65535
Outputs:
- commutator: float32 [12288, 12288], P('row', 'col')
The draws below stay inside these ranges and needn't reach their ends.
Inputs may be any that keep to these rules, and one draw needn't show every extreme that they name: `fock_matrix`: symmetric. `density_matrix`: symmetric. `fock_blocks`: symmetric 0/1 table of occupied blocks; every block on the diagonal is occupied. `density_blocks`: symmetric 0/1 table of occupied blocks; every block on the diagonal is occupied.
All inputs are finite; a program needn't handle non-finite values.
Results may differ from the reference program's by a relative error of at most 0.00035.
Values may be sent and summed in bfloat16 or wider, within the bound.
A program may use at most 64 MiB of HBM per device.

```python
import jax
import jax.numpy as jnp
from jax import lax

TILE = 768
BLK = 128
GRID = 16
ORDER = 12288
NBLK = 96
STEPS = 4


def mirrored(values):
    return (values + values.T) * 0.7071067811865476


def occupancy(key):
    key_levels, key_roll = jax.random.split(key)
    tile_level = jax.random.randint(key_levels, (GRID, GRID), 1, 5)
    tile_index = jnp.arange(GRID)
    tile_level = jnp.where(tile_index[:, None] <= tile_index[None, :], tile_level, tile_level.T)
    per_tile = TILE // BLK
    block_level = jnp.repeat(jnp.repeat(tile_level, per_tile, axis=0), per_tile, axis=1)
    block_roll = jax.random.randint(key_roll, (NBLK, NBLK), 0, 5)
    block_index = jnp.arange(NBLK)
    upper_side = block_index[:, None] <= block_index[None, :]
    block_roll = jnp.where(upper_side, block_roll, block_roll.T)
    occupied = (block_roll < block_level) | (block_index[:, None] == block_index[None, :])
    return occupied.astype(jnp.int32)


def draw_fock_matrix(key, part):
    key = jax.random.fold_in(key, 11)
    key_values, key_scales = jax.random.split(key)
    values = jax.random.truncated_normal(key_values, -4.0, 4.0, (ORDER, ORDER), jnp.float32)
    scales = jnp.exp(jax.random.uniform(key_scales, (ORDER,), jnp.float32, 0.0, 0.2))
    return (mirrored(values) * scales[:, None] * scales[None, :]).astype(jnp.bfloat16)


def draw_density_matrix(key, part):
    key = jax.random.fold_in(key, 12)
    key_values, key_scales = jax.random.split(key)
    values = jax.random.truncated_normal(key_values, -4.0, 4.0, (ORDER, ORDER), jnp.float32)
    scales = jnp.exp(jax.random.uniform(key_scales, (ORDER,), jnp.float32, 0.0, 0.2))
    return (mirrored(values) * scales[:, None] * scales[None, :] * 0.03125).astype(jnp.bfloat16)


def draw_fock_blocks(key, part):
    key = jax.random.fold_in(key, 21)
    return occupancy(key)


def draw_density_blocks(key, part):
    key = jax.random.fold_in(key, 22)
    return occupancy(key)


def setup_inputs(seed: int = 0) -> dict:
    keys = jax.random.split(jax.random.key(seed), 6)
    return {
        "fock_matrix": draw_fock_matrix(jax.random.fold_in(keys[5], 71), 0),
        "density_matrix": draw_density_matrix(jax.random.fold_in(keys[5], 71), 0),
        "fock_blocks": draw_fock_blocks(jax.random.fold_in(keys[5], 71), 0),
        "density_blocks": draw_density_blocks(jax.random.fold_in(keys[5], 71), 0),
        "slab_offset": jax.random.randint(keys[4], (1,), 0, GRID * 4096).astype(jnp.int32),
    }


def masked_tiles(values, occupied):
    blocks = values.reshape(NBLK, BLK, NBLK, BLK) * occupied.astype(values.dtype)[:, None, :, None]
    return blocks.reshape(GRID, TILE, GRID, TILE)


def reference(fock_matrix, density_matrix, fock_blocks, density_blocks, slab_offset):
    fock_tiles = masked_tiles(fock_matrix, fock_blocks)
    density_tiles = masked_tiles(density_matrix, density_blocks)
    columns = jnp.arange(GRID, dtype=jnp.int32)
    window_start = slab_offset[0] % GRID

    def tile_row(row_index):
        row_tiles = fock_tiles[row_index]
        running = jnp.zeros((GRID, TILE, TILE), jnp.float32)
        for offset_step in range(STEPS):
            inner = ((row_index + columns + window_start + offset_step) % GRID).astype(jnp.int32)
            left_tiles = jnp.take(row_tiles, inner, axis=1).astype(jnp.float32)
            right_tiles = density_tiles[inner, :, columns, :].astype(jnp.float32)
            running = running + jnp.einsum("ajc,jcb->jab", left_tiles, right_tiles, precision=lax.Precision.HIGHEST)
        return running

    product = lax.map(tile_row, jnp.arange(GRID, dtype=jnp.int32))
    product = product.transpose(0, 2, 1, 3).reshape(ORDER, ORDER)
    return product - product.T
```

```python
import functools

import jax
import jax.numpy as jnp
import numpy as np
from jax import lax
from jax.experimental import pallas as pl
from jax.experimental.pallas import tpu as pltpu
from jax.sharding import PartitionSpec as P

BLK = 128
GRID = 16
HALF = 384
TILE = 768
CUTS = 2
PIECE = HALF // CUTS
HOPS = 6
STEPS = 8
SWAPPED, OWN = 12, 13
CROSS, LAST = 7, 8
WIDTH = 256
MESH = pl.DeviceIdType.MESH


def div(a, b):
    return a // b if isinstance(a, int) else lax.div(a, np.int32(b))


def rem(a, b):
    return a % b if isinstance(a, int) else lax.rem(a, np.int32(b))


def where(cond, a, b):
    if isinstance(cond, bool):
        return a if cond else b
    return jnp.where(cond, a, b)


def flag(cond):
    return where(cond, 1, 0)


def differ(a, b):
    return a + b - 2 * a * b


class RowRoute:
    def __init__(self, i, y, off):
        t = rem(i + off, GRID)
        base = rem(t + 2, 8) - 2
        flip = rem(div(t + 2, 8), 2)
        first = (
            where(base <= 3, 4, 0),
            where(base == 0, 3, where(base == 1, 2, where(base == 4, 2, flag(base == 5)))),
        )
        self.y = y
        self.flip = (flip, where(base < 0, flip, 1 - flip))
        self.low = (where(base < 0, 0, base), where(base < 0, 1, 5 - base))
        self.swap = where(base <= 0, flip, where(base == 5, 1 - flip, 0))
        self.start = tuple(self.swap * f for f in self.flip)
        self.hops, self.slot = [], []
        for a in first:
            down = where(base < 0, base + 3, where(a > 0, base + a - 1, 0))
            up = where(base < 0, -base, where(a < 4, 8 - base - a, 0))
            self.hops.append((down, up))
            slots = []
            for s in range(4):
                d = base + s
                from_down = where(base < 0, flag(d >= 0), flag(s < a))
                hop = where(from_down == 1, d, where(base < 0, -d, 8 - d))
                turned = where(from_down == 1, self.flip[0], self.flip[1])
                moved = where(from_down == 1, hop - 1, hop + HOPS - 1)
                slots.append(where(hop == 0, OWN - turned, moved))
            self.slot.append(slots)
        self.both = tuple(flag(self.hops[0][w] * self.hops[1][w] > 0) for w in (0, 1))

    def crosses(self, way, h):
        source = rem(self.y + h, 8) if way == 0 else 7 - rem(self.y + 8 - h, 8)
        low, flip = self.low[way], self.flip[way]

        def turned(hop):
            return differ(flip, flag(where(hop > low, hop, low) > source))

        return differ(where(h == 0, self.start[way], turned(h)), turned(h + 1))


class ColRoute:
    def __init__(self, j, x_hi, off):
        t = rem(j + off, GRID)
        odd = rem(t, 2)
        u = rem(div(t + odd, 2), 8)
        self.down = (
            flag(u <= 3),
            where(u <= 1, 1, where(u == 4, 1, where(u == 2, odd, where(u == 5, odd, 0)))),
        )
        self.last_down = (where(u == 3, 1, where(u == 4, 0, 1 - odd)), 1 - odd)
        self.same = flag(self.down[0] == self.down[1])
        self.hops = [where(n == 1, u + 1, 8 - u) for n in self.down]
        self.need = [
            (where(n == 1, u, 8 - u), where(n == 1, u + 1, 7 - u)) for n in self.down
        ]
        self.hop_in, self.hop_out, self.slot = [], [], []
        for n, last, need in zip(self.down, self.last_down, self.need):
            w_in = u + x_hi - odd + 1 - last
            w_out = u + 1 - x_hi - odd + 1 - last
            self.hop_in.append(where(n == 1, w_in, 8 - w_in))
            self.hop_out.append(where(n == 1, w_out, 8 - w_out))
            low, high = LAST - last, CROSS + last
            self.slot.append([
                where(odd == 0, need[0], low), where(odd == 1, need[0], low),
                where(odd == 0, need[1], high), where(odd == 1, need[1], high),
            ])


def pick(values, s):
    out = values[-1]
    for n in range(len(values) - 2, -1, -1):
        out = jnp.where(s == n, values[n], out)
    return out


def kernel(
    off, fock_ref, density_ref, out_ref, rows, cols,
    load_sem, row_send, row_recv, swap_send, swap_recv, col_send, col_recv,
    x_send, x_recv, last_send, last_recv, pair_send, pair_recv,
):
    r, c = lax.axis_index("row"), lax.axis_index("col")
    core, x_hi, z = rem(r, 2), rem(div(r, 2), 2), div(r, 4)
    x_lo, y = div(c, 8), rem(c, 8)
    row, col = RowRoute(div(r, 2), y, off), ColRoute(c, x_hi, off)
    y_next = (rem(y + 7, 8), rem(y + 1, 8))
    z_next = (rem(r + 28, 32), rem(r + 4, 32))
    swap_dev = (r, (1 - x_lo) * 8 + y)
    x_dev = (r + 2 - 4 * x_hi, c)
    pair_dev = (r + 1 - 2 * core, c)
    mine = core * HALF
    other = HALF - mine

    loads = []
    for m, ref in enumerate((fock_ref, density_ref)):
        loads.append(pltpu.make_async_copy(ref, rows.at[m, OWN], load_sem.at[m, 0]))
        target = cols.at[m, 0, pl.ds(pl.multiple_of(mine, HALF), HALF)]
        loads.append(pltpu.make_async_copy(ref, target, load_sem.at[m, 1]))
    for load in loads:
        load.start()

    greet = [swap_dev, x_dev, pair_dev, (z_next[0], c), (z_next[1], c)]
    greet += [(r, x * 8 + v) for x in (0, 1) for v in y_next]
    barrier = pltpu.get_barrier_semaphore()
    for dev in greet:
        pl.semaphore_signal(barrier, inc=1, device_id=dev, device_id_type=MESH)
    pl.semaphore_wait(barrier, len(greet))

    def remote(src, dst, send, recv, dev):
        return pltpu.make_async_remote_copy(
            src_ref=src, dst_ref=dst, send_sem=send, recv_sem=recv,
            device_id=dev, device_id_type=MESH,
        )

    def row_part(m, slot, q):
        return rows.at[m, slot, pl.ds(q * PIECE, PIECE)]

    def col_part(m, slot, q, base):
        return cols.at[m, slot, pl.ds(pl.multiple_of(base + q * PIECE, PIECE), PIECE)]

    def row_copy(m, way, h, q):
        if isinstance(h, int):
            slot = OWN - row.start[way]
        else:
            slot = where(h == 0, OWN - row.start[way], h - 1 + way * HOPS)
        dev = (r, differ(x_lo, row.crosses(way, h)) * 8 + y_next[way])
        return remote(
            row_part(m, slot, q), row_part(m, h + way * HOPS, q),
            row_send.at[m, way, h, q], row_recv.at[m, way, h, q], dev,
        )

    def swap_copy(m, q):
        return remote(
            row_part(m, OWN, q), row_part(m, SWAPPED, q),
            swap_send.at[m, q], swap_recv.at[m, q], swap_dev,
        )

    def col_copy(m, h, q):
        dev = (where(col.down[m] == 1, z_next[0], z_next[1]), c)
        return remote(
            col_part(m, h, q, mine), col_part(m, h + 1, q, mine),
            col_send.at[m, h, q], col_recv.at[m, h, q], dev,
        )

    def x_copy(m, q):
        return remote(
            col_part(m, col.hop_out[m], q, mine), col_part(m, CROSS, q, mine),
            x_send.at[m, q], x_recv.at[m, q], x_dev,
        )

    def last_copy(m, q):
        dev = (where(col.last_down[m] == 1, z_next[0], z_next[1]), c)
        return remote(
            col_part(m, CROSS, q, mine), col_part(m, LAST, q, mine),
            last_send.at[m, q], last_recv.at[m, q], dev,
        )

    def pair_copy(m, slot, q, base):
        part = col_part(m, slot, q, base)
        return remote(part, part, pair_send.at[m, slot, q], pair_recv.at[m, slot, q], pair_dev)

    def row_arrived(m, way, h, q):
        @pl.when(h < row.hops[m][way])
        def _():
            row_copy(m, way, h, q).start()

    def col_arrived(m, h, q):
        @pl.when(h < col.hops[m])
        def _():
            col_copy(m, h, q).start()

        @pl.when(h == col.hop_out[m])
        def _():
            x_copy(m, q).start()

        @pl.when(jnp.logical_or(h == col.need[m][0], h == col.need[m][1]))
        def _():
            pair_copy(m, h, q, mine).start()

    for load in loads:
        load.wait()
    for q in range(CUTS):
        for m in (0, 1):
            @pl.when(row.swap == 1)
            def _():
                swap_copy(m, q).start()

            for way in (0, 1):
                @pl.when(row.start[way] == 0)
                def _():
                    row_arrived(m, way, 0, q)

            col_arrived(m, 0, q)
    for q in range(CUTS):
        for m in (0, 1):
            @pl.when(row.swap == 1)
            def _():
                swap_copy(m, q).wait_recv()
                for way in (0, 1):
                    @pl.when(row.start[way] == 1)
                    def _():
                        row_arrived(m, way, 0, q)

    def turn(m, shared, step):
        odd = rem(step, 2)
        hop = where(shared == 1, div(step + 1 - m, 2), step)
        ours = where(shared == 1, flag(odd == 1 - m), 1)
        return hop, ours

    @pl.loop(1, STEPS + 1)
    def _(step):
        for q in range(CUTS):
            for way in (0, 1):
                for m in (0, 1):
                    h, ours = turn(m, row.both[way], step)

                    @pl.when((ours == 1) & (h >= 1) & (h <= row.hops[m][way]))
                    def _():
                        row_copy(m, way, h - 1, q).wait_recv()
                        row_arrived(m, way, h, q)

            for m in (0, 1):
                h, ours = turn(m, col.same, step)

                @pl.when((ours == 1) & (h >= 1) & (h <= col.hops[m]))
                def _():
                    col_copy(m, h - 1, q).wait_recv()
                    col_arrived(m, h, q)

            for m in (0, 1):
                h = col.hop_in[m]
                due = where(col.same == 1, where(h == 0, 0, 2 * h - 1 + m), h)

                @pl.when(step == due + 1)
                def _():
                    x_copy(m, q).wait_recv()
                    last_copy(m, q).start()
                    pair_copy(m, CROSS, q, mine).start()

                @pl.when(step == due + 2)
                def _():
                    last_copy(m, q).wait_recv()
                    pair_copy(m, LAST, q, mine).start()

    for m in (0, 1):
        for q in range(CUTS):
            for slot in (col.need[m][0], col.need[m][1], CROSS, LAST):
                pair_copy(m, slot, q, other).wait_recv()

    out_ref[...] = jnp.zeros_like(out_ref)

    @pl.loop(0, 4)
    def _(s):
        row_slot = [pick(row.slot[m], s) for m in (0, 1)]
        col_slot = [pick(col.slot[m], s) for m in (0, 1)]

        @pl.loop(0, TILE // WIDTH)
        def _(n):
            span = pl.ds(pl.multiple_of(n * WIDTH, WIDTH), WIDTH)
            fp = jnp.dot(
                rows[0, row_slot[0]], cols[1, col_slot[1], :, span],
                preferred_element_type=jnp.float32,
            )
            pf = jnp.dot(
                rows[1, row_slot[1]], cols[0, col_slot[0], :, span],
                preferred_element_type=jnp.float32,
            )
            out_ref[:, span] += fp - pf

    for m in (0, 1):
        for q in range(CUTS):
            @pl.when(row.swap == 1)
            def _():
                swap_copy(m, q).wait_send()

            x_copy(m, q).wait_send()
            last_copy(m, q).wait_send()
            for slot in (col.need[m][0], col.need[m][1], CROSS, LAST):
                pair_copy(m, slot, q, mine).wait_send()

    @pl.loop(0, HOPS)
    def _(h):
        for m in (0, 1):
            for q in range(CUTS):
                for way in (0, 1):
                    @pl.when(h < row.hops[m][way])
                    def _():
                        row_copy(m, way, h, q).wait_send()

                @pl.when(h < col.hops[m])
                def _():
                    col_copy(m, h, q).wait_send()


def commute(fock, density, off):
    sems = [(2, 2)] + [(2, 2, HOPS, CUTS)] * 2 + [(2, CUTS)] * 2
    sems += [(2, HOPS, CUTS)] * 2 + [(2, CUTS)] * 4 + [(2, 9, CUTS)] * 2
    return pl.pallas_call(
        functools.partial(kernel, off),
        out_shape=jax.ShapeDtypeStruct((HALF, TILE), jnp.float32),
        in_specs=[pl.BlockSpec(memory_space=pl.ANY)] * 2,
        out_specs=pl.BlockSpec(memory_space=pltpu.VMEM),
        scratch_shapes=[
            pltpu.VMEM((2, 14, HALF, TILE), jnp.bfloat16),
            pltpu.VMEM((2, 9, TILE, TILE), jnp.bfloat16),
        ] + [pltpu.SemaphoreType.DMA(shape) for shape in sems],
        compiler_params=pltpu.CompilerParams(
            collective_id=off, has_side_effects=True, vmem_limit_bytes=52 << 20
        ),
    )(fock, density)


def masked_piece(values, occupied, first_row, first_col):
    row_blocks = values.shape[0] // BLK
    col_blocks = values.shape[1] // BLK
    window = lax.dynamic_slice(occupied, (first_row, first_col), (row_blocks, col_blocks))
    blocks = (
        values.reshape(row_blocks, BLK, col_blocks, BLK)
        * window.astype(values.dtype)[:, None, :, None]
    )
    return blocks.reshape(values.shape)


def shards(fock_matrix, density_matrix, fock_blocks, density_blocks, slab_offset):
    corner = (lax.axis_index("row") * (HALF // BLK), lax.axis_index("col") * (TILE // BLK))
    fock = masked_piece(fock_matrix, fock_blocks, *corner)
    density = masked_piece(density_matrix, density_blocks, *corner)
    branches = [functools.partial(commute, off=off) for off in range(GRID)]
    return lax.switch(slab_offset[0] % GRID, branches, fock, density)


def solution(mesh):
    placed = (P("row", "col"), P("row", "col"), P(), P(), P())
    return jax.shard_map(
        shards, mesh=mesh, in_specs=placed, out_specs=P("row", "col"), check_vma=False
    )
```

```python
import functools

import jax
import jax.numpy as jnp
import numpy as np
from jax import lax
from jax.experimental import pallas as pl
from jax.experimental.pallas import tpu as pltpu
from jax.sharding import PartitionSpec as P

BLK = 128
GRID = 16
HALF = 384
TILE = 768
WINDOW = 4
CUTS = 4
PIECE = TILE // CUTS
LOWER = CUTS // 2
HOPS = 6
LAG = 2
STEPS = 6 + 2 * LAG
SWAPPED, OWN = 12, 13
CROSS, LAST = 7, 8
GOT = 14
WIDTH = 256
MESH = pl.DeviceIdType.MESH


def div(a, b):
    return a // b if isinstance(a, int) else lax.div(a, np.int32(b))


def rem(a, b):
    return a % b if isinstance(a, int) else lax.rem(a, np.int32(b))


def where(cond, a, b):
    if isinstance(cond, bool):
        return a if cond else b
    return jnp.where(cond, a, b)


def flag(cond):
    return where(cond, 1, 0)


def differ(a, b):
    return a + b - 2 * a * b


class RowRoute:
    def __init__(self, i, y, off):
        t = rem(i + off, GRID)
        base = rem(t + 2, 8) - 2
        flip = rem(div(t + 2, 8), 2)
        first = (
            where(base <= 3, 4, 0),
            where(base == 0, 3, where(base == 1, 2, where(base == 4, 2, flag(base == 5)))),
        )
        self.y = y
        self.flip = (flip, where(base < 0, flip, 1 - flip))
        self.low = (where(base < 0, 0, base), where(base < 0, 1, 5 - base))
        self.swap = where(base <= 0, flip, where(base == 5, 1 - flip, 0))
        self.zero = flag((base <= 0) | (base == 5)) * (1 - self.swap)
        self.zero_s = where(base == 5, 3, where(base < 0, -base, 0))
        self.base, self.far = base, where(base < 0, 0, 8)
        self.start = tuple(self.swap * f * flag(base < 0) for f in self.flip)
        self.hops, self.slot = [], []
        for a in first:
            down = where(base < 0, base + 3, where(a > 0, base + a - 1, 0))
            up = where(base < 0, -base, where(a < 4, 8 - base - a, 0))
            self.hops.append((down, up))
            slots = []
            for s in range(4):
                d = base + s
                from_down = where(base < 0, flag(d >= 0), flag(s < a))
                hop = where(from_down == 1, d, where(base < 0, -d, 8 - d))
                turned = where(from_down == 1, self.flip[0], self.flip[1])
                moved = where(from_down == 1, hop - 1, hop + HOPS - 1)
                slots.append(where(hop == 0, OWN - turned, moved))
            self.slot.append(slots)
        self.both = tuple(flag(self.hops[0][w] * self.hops[1][w] > 0) for w in (0, 1))

    def step_of(self, way, h):
        return h - self.base if way == 0 else self.far - h - self.base

    def crosses(self, way, h):
        source = rem(self.y + h, 8) if way == 0 else 7 - rem(self.y + 8 - h, 8)
        low, flip = self.low[way], self.flip[way]

        def turned(hop):
            return differ(flip, flag(where(hop > low, hop, low) > source))

        return differ(where(h == 0, self.start[way], turned(h)), turned(h + 1))


class ColRoute:
    def __init__(self, j, x_hi, off):
        t = rem(j + off, GRID)
        odd = rem(t, 2)
        u = rem(div(t + odd, 2), 8)
        self.down = (
            flag(u <= 3),
            where(u <= 1, 1, where(u == 4, 1, where(u == 2, odd, where(u == 5, odd, 0)))),
        )
        self.last_down = (where(u == 3, 1, where(u == 4, 0, 1 - odd)), 1 - odd)
        self.same = flag(self.down[0] == self.down[1])
        self.hops = [where(n == 1, u + 1, 8 - u) for n in self.down]
        self.need = [
            (where(n == 1, u, 8 - u), where(n == 1, u + 1, 7 - u)) for n in self.down
        ]
        self.cross_s = [3 - odd - 2 * last for last in self.last_down]
        self.last_s = [1 - odd + 2 * last for last in self.last_down]
        self.odd = odd
        self.hop_in, self.hop_out, self.slot = [], [], []
        for n, last, need in zip(self.down, self.last_down, self.need):
            w_in = u + x_hi - odd + 1 - last
            w_out = u + 1 - x_hi - odd + 1 - last
            self.hop_in.append(where(n == 1, w_in, 8 - w_in))
            self.hop_out.append(where(n == 1, w_out, 8 - w_out))
            low, high = LAST - last, CROSS + last
            self.slot.append([
                where(odd == 0, need[0], low), where(odd == 1, need[0], low),
                where(odd == 0, need[1], high), where(odd == 1, need[1], high),
            ])


def pick(values, s):
    out = values[-1]
    for n in range(len(values) - 2, -1, -1):
        out = jnp.where(s == n, values[n], out)
    return out


def kernel(
    off, fock_ref, density_ref, out_ref, tiles,
    load_sem, give_send, give_recv, row_send, row_recv, swap_send, swap_recv,
    col_send, col_recv, x_send, x_recv, last_send, last_recv, pair_send, pair_recv,
):
    r, c = lax.axis_index("row"), lax.axis_index("col")
    core, x_hi, z = rem(r, 2), rem(div(r, 2), 2), div(r, 4)
    x_lo, y = div(c, 8), rem(c, 8)
    row, col = RowRoute(div(r, 2), y, off), ColRoute(c, x_hi, off)
    y_next = (rem(y + 7, 8), rem(y + 1, 8))
    z_next = (rem(r + 28, 32), rem(r + 4, 32))
    swap_dev = (r, (1 - x_lo) * 8 + y)
    x_dev = (r + 2 - 4 * x_hi, c)
    pair_dev = (r + 1 - 2 * core, c)
    refs = (fock_ref, density_ref)
    early = (row.start[0] + row.start[1]) > 0
    late = (row.swap == 1) & ((row.start[0] + row.start[1]) == 0)

    home = where(core == 0, OWN, 0)
    away = where(core == 0, 0, OWN)
    mine = pl.ds(pl.multiple_of(core * HALF, HALF), HALF)
    other = pl.ds(pl.multiple_of(HALF - core * HALF, HALF), HALF)

    def load(m):
        return pltpu.make_async_copy(refs[m], tiles.at[m, home, mine], load_sem.at[m, 0])

    def keep(m):
        target = tiles.at[m, GOT + row.zero_s, pl.ds(0, HALF)]
        return pltpu.make_async_copy(refs[m], target, load_sem.at[m, 1])

    def remote(src, dst, send, recv, dev):
        return pltpu.make_async_remote_copy(
            src_ref=src, dst_ref=dst, send_sem=send, recv_sem=recv,
            device_id=dev, device_id_type=MESH,
        )

    def give(m):
        return remote(
            refs[m], tiles.at[m, away, mine], give_send.at[m], give_recv.at[m], pair_dev
        )

    def taken(m):
        return remote(
            refs[m], tiles.at[m, home, other], give_send.at[m], give_recv.at[m], pair_dev
        )

    for m in (0, 1):
        load(m).start()

    @pl.when((core == 1) & (row.zero == 1))
    def _():
        for m in (0, 1):
            keep(m).start()

    greet = [swap_dev, x_dev, pair_dev, (z_next[0], c), (z_next[1], c)]
    greet += [(r, x * 8 + v) for x in (0, 1) for v in y_next]
    barrier = pltpu.get_barrier_semaphore()
    for dev in greet:
        pl.semaphore_signal(barrier, inc=1, device_id=dev, device_id_type=MESH)
    pl.semaphore_wait(barrier, len(greet))

    def part(m, slot, q):
        return tiles.at[m, slot, pl.ds(q * PIECE, PIECE)]

    def row_copy(m, way, h, q):
        if isinstance(h, int):
            slot = OWN - row.start[way]
        else:
            slot = where(h == 0, OWN - row.start[way], h - 1 + way * HOPS)
        dev = (r, differ(x_lo, row.crosses(way, h)) * 8 + y_next[way])
        return remote(
            part(m, slot, q), part(m, h + way * HOPS, q),
            row_send.at[m, way, h, q], row_recv.at[m, way, h, q], dev,
        )

    def swap_copy(m, q):
        return remote(
            part(m, OWN, q), part(m, SWAPPED, q),
            swap_send.at[m, q], swap_recv.at[m, q], swap_dev,
        )

    def col_copy(m, h, q):
        dev = (where(col.down[m] == 1, z_next[0], z_next[1]), c)
        return remote(
            part(m, h, q), part(m, h + 1, q),
            col_send.at[m, h, q], col_recv.at[m, h, q], dev,
        )

    def x_copy(m, q):
        return remote(
            part(m, col.hop_out[m], q), part(m, CROSS, q),
            x_send.at[m, q], x_recv.at[m, q], x_dev,
        )

    def last_copy(m, q):
        dev = (where(col.last_down[m] == 1, z_next[0], z_next[1]), c)
        return remote(
            part(m, CROSS, q), part(m, LAST, q),
            last_send.at[m, q], last_recv.at[m, q], dev,
        )

    def pair_copy(m, slot, s, q, to):
        return remote(
            part(m, slot, q), part(m, GOT + s, to),
            pair_send.at[m, s, to], pair_recv.at[m, s, to], pair_dev,
        )

    def row_pair(m, slot, s, q):
        if q >= LOWER:
            pair_copy(m, slot, s, q, q - LOWER).start()

    def row_go(m, way, h, q):
        @pl.when(h < row.hops[m][way])
        def _():
            row_copy(m, way, h, q).start()

    def row_arrived(m, way, h, q):
        row_go(m, way, h, q)

        @pl.when(h >= row.low[way])
        def _():
            row_pair(m, h - 1 + way * HOPS, row.step_of(way, h), q)

    def col_arrived(m, h, q):
        @pl.when(h < col.hops[m])
        def _():
            col_copy(m, h, q).start()

        @pl.when(h == col.hop_out[m])
        def _():
            x_copy(m, q).start()

        for n in (0, 1):
            @pl.when(h == col.need[m][n])
            def _():
                pair_copy(m, h, col.odd + 2 * n, q, q).start()

    def turn(m, shared, step):
        odd = rem(step, 2)
        hop = where(shared == 1, div(step + 1 - m, 2), step)
        ours = where(shared == 1, flag(odd == 1 - m), 1)
        return hop, ours

    for m in (0, 1):
        give(m).start()

    @pl.when(core == 0)
    def _():
        for q in range(CUTS):
            for m in (0, 1):
                if q == 0:
                    load(m).wait()
                if q == LOWER:
                    taken(m).wait_recv()

                @pl.when(early)
                def _():
                    swap_copy(m, q).start()

                for way in (0, 1):
                    @pl.when(row.start[way] == 0)
                    def _():
                        row_go(m, way, 0, q)

        for q in range(CUTS):
            for m in (0, 1):
                @pl.when(late)
                def _():
                    swap_copy(m, q).start()

                @pl.when(early)
                def _():
                    swap_copy(m, q).wait_recv()
                    row_pair(m, SWAPPED, row.zero_s, q)
                    for way in (0, 1):
                        @pl.when(row.start[way] == 1)
                        def _():
                            row_go(m, way, 0, q)

        @pl.loop(1, HOPS + 2)
        def _(step):
            for q in range(CUTS):
                for way in (0, 1):
                    for m in (0, 1):
                        h, ours = turn(m, row.both[way], step)

                        @pl.when((ours == 1) & (h >= 1) & (h <= row.hops[m][way]))
                        def _():
                            row_copy(m, way, h - 1, q).wait_recv()
                            row_arrived(m, way, h, q)

        for m in (0, 1):
            for q in range(CUTS):
                @pl.when(late)
                def _():
                    swap_copy(m, q).wait_recv()
                    row_pair(m, SWAPPED, row.zero_s, q)

        @pl.loop(0, WINDOW)
        def _(s):
            for m in (0, 1):
                for q in range(CUTS):
                    pair_copy(m, GOT + s, s, q, q).wait_recv()

    @pl.when(core == 1)
    def _():
        for q in range(CUTS):
            for m in (0, 1):
                if q == 0:
                    taken(m).wait_recv()
                if q == LOWER:
                    load(m).wait()
                col_arrived(m, 0, q)

        @pl.loop(1, STEPS + 1)
        def _(step):
            for q in range(CUTS):
                for m in (0, 1):
                    h, ours = turn(m, col.same, step)

                    @pl.when((ours == 1) & (h >= 1) & (h <= col.hops[m]))
                    def _():
                        col_copy(m, h - 1, q).wait_recv()
                        col_arrived(m, h, q)

                for m in (0, 1):
                    h = col.hop_in[m]
                    due = where(col.same == 1, where(h == 0, 0, 2 * h - 1 + m), h)

                    @pl.when(step == due + LAG)
                    def _():
                        x_copy(m, q).wait_recv()
                        last_copy(m, q).start()
                        pair_copy(m, CROSS, col.cross_s[m], q, q).start()

                    @pl.when(step == due + 2 * LAG)
                    def _():
                        last_copy(m, q).wait_recv()
                        pair_copy(m, LAST, col.last_s[m], q, q).start()

        @pl.loop(0, WINDOW)
        def _(s):
            @pl.when((row.zero == 0) | (s != row.zero_s))
            def _():
                for m in (0, 1):
                    for q in range(LOWER):
                        pair_copy(m, GOT + s, s, q, q).wait_recv()

        @pl.when(row.zero == 1)
        def _():
            for m in (0, 1):
                keep(m).wait()

    out_ref[...] = jnp.zeros_like(out_ref)

    @pl.loop(0, WINDOW)
    def _(s):
        left = [where(core == 0, pick(row.slot[m], s), GOT + s) for m in (0, 1)]
        right = [where(core == 0, GOT + s, pick(col.slot[m], s)) for m in (0, 1)]

        @pl.loop(0, TILE // WIDTH)
        def _(n):
            span = pl.ds(pl.multiple_of(n * WIDTH, WIDTH), WIDTH)
            fp = jnp.dot(
                tiles[0, left[0], :HALF], tiles[1, right[1], :, span],
                preferred_element_type=jnp.float32,
            )
            pf = jnp.dot(
                tiles[1, left[1], :HALF], tiles[0, right[0], :, span],
                preferred_element_type=jnp.float32,
            )
            out_ref[:, span] += fp - pf

    for m in (0, 1):
        give(m).wait_send()

    @pl.when(core == 0)
    def _():
        @pl.when(row.swap == 1)
        def _():
            for m in (0, 1):
                for q in range(CUTS):
                    swap_copy(m, q).wait_send()

        @pl.loop(0, HOPS)
        def _(h):
            for m in (0, 1):
                for way in (0, 1):
                    @pl.when(h < row.hops[m][way])
                    def _():
                        for q in range(CUTS):
                            row_copy(m, way, h, q).wait_send()

        @pl.loop(0, WINDOW)
        def _(s):
            @pl.when((row.zero == 0) | (s != row.zero_s))
            def _():
                for m in (0, 1):
                    for q in range(LOWER):
                        pair_copy(m, GOT + s, s, q, q).wait_send()

    @pl.when(core == 1)
    def _():
        for m in (0, 1):
            for q in range(CUTS):
                x_copy(m, q).wait_send()
                last_copy(m, q).wait_send()

        @pl.loop(0, HOPS)
        def _(h):
            for m in (0, 1):
                @pl.when(h < col.hops[m])
                def _():
                    for q in range(CUTS):
                        col_copy(m, h, q).wait_send()

        @pl.loop(0, WINDOW)
        def _(s):
            for m in (0, 1):
                for q in range(CUTS):
                    pair_copy(m, GOT + s, s, q, q).wait_send()


def commute(fock, density, off):
    sems = [(2, 2)] + [(2,)] * 2 + [(2, 2, HOPS, CUTS)] * 2 + [(2, CUTS)] * 2
    sems += [(2, HOPS, CUTS)] * 2 + [(2, CUTS)] * 4 + [(2, WINDOW, CUTS)] * 2
    return pl.pallas_call(
        functools.partial(kernel, off),
        out_shape=jax.ShapeDtypeStruct((HALF, TILE), jnp.float32),
        in_specs=[pl.BlockSpec(memory_space=pl.ANY)] * 2,
        out_specs=pl.BlockSpec(memory_space=pltpu.VMEM),
        scratch_shapes=[
            pltpu.VMEM((2, GOT + WINDOW, TILE, TILE), jnp.bfloat16),
        ] + [pltpu.SemaphoreType.DMA(shape) for shape in sems],
        compiler_params=pltpu.CompilerParams(
            collective_id=off, has_side_effects=True, vmem_limit_bytes=52 << 20
        ),
    )(fock, density)


def masked_piece(values, occupied, first_row, first_col):
    row_blocks = values.shape[0] // BLK
    col_blocks = values.shape[1] // BLK
    window = lax.dynamic_slice(occupied, (first_row, first_col), (row_blocks, col_blocks))
    blocks = (
        values.reshape(row_blocks, BLK, col_blocks, BLK)
        * window.astype(values.dtype)[:, None, :, None]
    )
    return blocks.reshape(values.shape)


def shards(fock_matrix, density_matrix, fock_blocks, density_blocks, slab_offset):
    corner = (lax.axis_index("row") * (HALF // BLK), lax.axis_index("col") * (TILE // BLK))
    fock = masked_piece(fock_matrix, fock_blocks, *corner)
    density = masked_piece(density_matrix, density_blocks, *corner)
    branches = [functools.partial(commute, off=off) for off in range(GRID)]
    return lax.switch(slab_offset[0] % GRID, branches, fock, density)


def solution(mesh):
    placed = (P("row", "col"), P("row", "col"), P(), P(), P())
    return jax.shard_map(
        shards, mesh=mesh, in_specs=placed, out_specs=P("row", "col"), check_vma=False
    )
```

```python
import functools

import jax
import jax.numpy as jnp
import numpy as np
from jax import lax
from jax.experimental import pallas as pl
from jax.experimental.pallas import tpu as pltpu
from jax.sharding import PartitionSpec as P

BLK = 128
GRID = 16
HALF = 384
TILE = 768
WINDOW = 4
CUTS = 4
PIECE = TILE // CUTS
LOWER = CUTS // 2
HOPS = 6
LAG = 2
STEPS = 6 + 2 * LAG
SWAPPED, OWN = 12, 13
CROSS, LAST = 7, 8
GOT = 14
WIDTH = 256
MESH = pl.DeviceIdType.MESH


def div(a, b):
    return a // b if isinstance(a, int) else lax.div(a, np.int32(b))


def rem(a, b):
    return a % b if isinstance(a, int) else lax.rem(a, np.int32(b))


def where(cond, a, b):
    if isinstance(cond, bool):
        return a if cond else b
    return jnp.where(cond, a, b)


def flag(cond):
    return where(cond, 1, 0)


def at(pair, n):
    return where(n == 0, pair[0], pair[1])


def differ(a, b):
    return a + b - 2 * a * b


class RowRoute:
    def __init__(self, i, y, off):
        t = rem(i + off, GRID)
        base = rem(t + 2, 8) - 2
        flip = rem(div(t + 2, 8), 2)
        first = (
            where(base <= 3, 4, 0),
            where(base == 0, 3, where(base == 1, 2, where(base == 4, 2, flag(base == 5)))),
        )
        self.y = y
        self.flip = (flip, where(base < 0, flip, 1 - flip))
        self.low = (where(base < 0, 0, base), where(base < 0, 1, 5 - base))
        self.swap = where(base <= 0, flip, where(base == 5, 1 - flip, 0))
        self.zero = flag((base <= 0) | (base == 5)) * (1 - self.swap)
        self.zero_s = where(base == 5, 3, where(base < 0, -base, 0))
        self.base, self.far = base, where(base < 0, 0, 8)
        self.start = tuple(
            flag(base < 0) * self.swap * self.first_turned(way) for way in (0, 1)
        )
        self.hops, self.slot = [], []
        for a in first:
            down = where(base < 0, base + 3, where(a > 0, base + a - 1, 0))
            up = where(base < 0, -base, where(a < 4, 8 - base - a, 0))
            self.hops.append((down, up))
            slots = []
            for s in range(4):
                d = base + s
                from_down = where(base < 0, flag(d >= 0), flag(s < a))
                hop = where(from_down == 1, d, where(base < 0, -d, 8 - d))
                turned = where(from_down == 1, self.flip[0], self.flip[1])
                moved = where(from_down == 1, hop - 1, hop + HOPS - 1)
                slots.append(where(hop == 0, OWN - turned, moved))
            self.slot.append(slots)
        self.both = tuple(flag(self.hops[0][w] * self.hops[1][w] > 0) for w in (0, 1))

    def step_of(self, way, h):
        return where(way == 0, h, self.far - h) - self.base

    def first_turned(self, way):
        source = self.y if way == 0 else 7 - self.y
        low = where(self.low[way] > 1, self.low[way], 1)
        return differ(self.flip[way], flag(low > source))

    def crosses(self, way, h):
        source = where(way == 0, rem(self.y + h, 8), 7 - rem(self.y + 8 - h, 8))
        low, flip = at(self.low, way), at(self.flip, way)
        now = differ(flip, flag(where(h > low, h, low) > source))
        new = differ(flip, flag(where(h + 1 > low, h + 1, low) > source))
        return differ(where(h == 0, at(self.start, way), now), new)


class ColRoute:
    def __init__(self, j, x_hi, off):
        t = rem(j + off, GRID)
        odd = rem(t, 2)
        u = rem(div(t + odd, 2), 8)
        self.down = (
            flag(u <= 3),
            where(u <= 1, 1, where(u == 4, 1, where(u == 2, odd, where(u == 5, odd, 0)))),
        )
        self.last_down = (where(u == 3, 1, where(u == 4, 0, 1 - odd)), 1 - odd)
        self.same = flag(self.down[0] == self.down[1])
        self.hops = [where(n == 1, u + 1, 8 - u) for n in self.down]
        self.need = [
            (where(n == 1, u, 8 - u), where(n == 1, u + 1, 7 - u)) for n in self.down
        ]
        self.cross_s = [3 - odd - 2 * last for last in self.last_down]
        self.last_s = [1 - odd + 2 * last for last in self.last_down]
        self.odd = odd
        self.hop_in, self.hop_out, self.slot = [], [], []
        for n, last, need in zip(self.down, self.last_down, self.need):
            w_in = u + x_hi - odd + 1 - last
            w_out = u + 1 - x_hi - odd + 1 - last
            self.hop_in.append(where(n == 1, w_in, 8 - w_in))
            self.hop_out.append(where(n == 1, w_out, 8 - w_out))
            low, high = LAST - last, CROSS + last
            self.slot.append([
                where(odd == 0, need[0], low), where(odd == 1, need[0], low),
                where(odd == 0, need[1], high), where(odd == 1, need[1], high),
            ])


def pick(values, s):
    out = values[-1]
    for n in range(len(values) - 2, -1, -1):
        out = jnp.where(s == n, values[n], out)
    return out


def kernel(
    off, fock_ref, density_ref, out_ref, tiles,
    load_sem, give_send, give_recv, row_send, row_recv, swap_send, swap_recv,
    col_send, col_recv, x_send, x_recv, last_send, last_recv, pair_send, pair_recv,
):
    r, c = lax.axis_index("row"), lax.axis_index("col")
    core, x_hi, z = rem(r, 2), rem(div(r, 2), 2), div(r, 4)
    x_lo, y = div(c, 8), rem(c, 8)
    row, col = RowRoute(div(r, 2), y, off), ColRoute(c, x_hi, off)
    y_next = (rem(y + 7, 8), rem(y + 1, 8))
    z_next = (rem(r + 28, 32), rem(r + 4, 32))
    swap_dev = (r, (1 - x_lo) * 8 + y)
    x_dev = (r + 2 - 4 * x_hi, c)
    pair_dev = (r + 1 - 2 * core, c)
    refs = (fock_ref, density_ref)
    early = (row.start[0] + row.start[1]) > 0
    late = (row.swap == 1) & ((row.start[0] + row.start[1]) == 0)

    home = where(core == 0, OWN, 0)
    away = where(core == 0, 0, OWN)
    mine = pl.ds(pl.multiple_of(core * HALF, HALF), HALF)
    other = pl.ds(pl.multiple_of(HALF - core * HALF, HALF), HALF)

    def load(m):
        return pltpu.make_async_copy(refs[m], tiles.at[m, home, mine], load_sem.at[m, 0])

    def keep(m):
        target = tiles.at[m, GOT + row.zero_s, pl.ds(0, HALF)]
        return pltpu.make_async_copy(refs[m], target, load_sem.at[m, 1])

    def remote(src, dst, send, recv, dev):
        return pltpu.make_async_remote_copy(
            src_ref=src, dst_ref=dst, send_sem=send, recv_sem=recv,
            device_id=dev, device_id_type=MESH,
        )

    def give(m):
        return remote(
            refs[m], tiles.at[m, away, mine], give_send.at[m], give_recv.at[m], pair_dev
        )

    def taken(m):
        return remote(
            refs[m], tiles.at[m, home, other], give_send.at[m], give_recv.at[m], pair_dev
        )

    for m in (0, 1):
        load(m).start()

    @pl.when((core == 1) & (row.zero == 1))
    def _():
        for m in (0, 1):
            keep(m).start()

    greet = [swap_dev, x_dev, pair_dev, (z_next[0], c), (z_next[1], c)]
    greet += [(r, x * 8 + v) for x in (0, 1) for v in y_next]
    barrier = pltpu.get_barrier_semaphore()
    for dev in greet:
        pl.semaphore_signal(barrier, inc=1, device_id=dev, device_id_type=MESH)
    pl.semaphore_wait(barrier, len(greet))

    def part(m, slot, q):
        return tiles.at[m, slot, pl.ds(pl.multiple_of(q * PIECE, PIECE), PIECE)]

    def row_copy(m, way, h, q):
        slot = where(h == 0, OWN - at(row.start, way), h - 1 + way * HOPS)
        dev = (r, differ(x_lo, row.crosses(way, h)) * 8 + at(y_next, way))
        return remote(
            part(m, slot, q), part(m, h + way * HOPS, q),
            row_send.at[m, way, h, q], row_recv.at[m, way, h, q], dev,
        )

    def row_hops(m, way):
        return where(m == 0, at(row.hops[0], way), at(row.hops[1], way))

    def swap_copy(m, q):
        return remote(
            part(m, OWN, q), part(m, SWAPPED, q),
            swap_send.at[m, q], swap_recv.at[m, q], swap_dev,
        )

    def col_copy(m, h, q):
        dev = (where(at(col.down, m) == 1, z_next[0], z_next[1]), c)
        return remote(
            part(m, h, q), part(m, h + 1, q),
            col_send.at[m, h, q], col_recv.at[m, h, q], dev,
        )

    def x_copy(m, q):
        return remote(
            part(m, at(col.hop_out, m), q), part(m, CROSS, q),
            x_send.at[m, q], x_recv.at[m, q], x_dev,
        )

    def last_copy(m, q):
        dev = (where(at(col.last_down, m) == 1, z_next[0], z_next[1]), c)
        return remote(
            part(m, CROSS, q), part(m, LAST, q),
            last_send.at[m, q], last_recv.at[m, q], dev,
        )

    def pair_copy(m, slot, s, q, to):
        return remote(
            part(m, slot, q), part(m, GOT + s, to),
            pair_send.at[m, s, to], pair_recv.at[m, s, to], pair_dev,
        )

    def turn(m, shared, step):
        odd = rem(step, 2)
        hop = where((shared == 1) & (step > 0), div(step + 1 - m, 2), step)
        ours = (shared == 0) | (step == 0) | (odd == 1 - m)
        return hop, ours

    for m in (0, 1):
        give(m).start()

    @pl.loop(0, HALF // 8)
    def _(n):
        out_ref[pl.ds(n * 8, 8)] = jnp.zeros((8, TILE), jnp.float32)

    for m in (0, 1):
        load(m).wait()

    @pl.when(core == 0)
    def _():
        @pl.loop(0, HOPS + 2)
        def _(step):
            @pl.loop(0, 4 * CUTS)
            def _(n):
                q, way, m = div(n, 4), rem(div(n, 2), 2), rem(n, 2)
                h, ours = turn(m, at(row.both, way), step)
                hops = row_hops(m, way)
                live = ours & (h <= hops)

                @pl.when((step == 0) & (n == 4 * LOWER))
                def _():
                    for k in (0, 1):
                        taken(k).wait_recv()

                @pl.when(early & (step == 0) & (way == 0))
                def _():
                    swap_copy(m, q).start()

                @pl.when(live & (h >= 1))
                def _():
                    row_copy(m, way, h - 1, q).wait_recv()

                @pl.when(live & (h < hops) & ((h >= 1) | (at(row.start, way) == 0)))
                def _():
                    row_copy(m, way, h, q).start()

                @pl.when(live & (h >= 1) & (h >= at(row.low, way)) & (q >= LOWER))
                def _():
                    slot = h - 1 + way * HOPS
                    pair_copy(m, slot, row.step_of(way, h), q, q - LOWER).start()

            @pl.when((step == 0) & (row.swap == 1))
            def _():
                @pl.loop(0, 2 * CUTS)
                def _(n):
                    q, m = div(n, 2), rem(n, 2)

                    @pl.when(late)
                    def _():
                        swap_copy(m, q).start()

                    @pl.when(early)
                    def _():
                        swap_copy(m, q).wait_recv()

                        @pl.loop(0, 2)
                        def _(way):
                            @pl.when((at(row.start, way) == 1) & (row_hops(m, way) > 0))
                            def _():
                                row_copy(m, way, 0, q).start()

            @pl.when((step == HOPS + 1) & (row.swap == 1))
            def _():
                @pl.loop(0, 2 * CUTS)
                def _(n):
                    q, m = div(n, 2), rem(n, 2)

                    @pl.when(late)
                    def _():
                        swap_copy(m, q).wait_recv()

                    @pl.when(q >= LOWER)
                    def _():
                        pair_copy(m, SWAPPED, row.zero_s, q, q - LOWER).start()

        @pl.loop(0, WINDOW)
        def _(s):
            @pl.loop(0, 2 * CUTS)
            def _(n):
                q, m = div(n, 2), rem(n, 2)
                pair_copy(m, GOT + s, s, q, q).wait_recv()

    @pl.when(core == 1)
    def _():
        for m in (0, 1):
            taken(m).wait_recv()

        @pl.loop(0, STEPS + 1)
        def _(step):
            @pl.loop(0, 2 * CUTS)
            def _(n):
                q, m = div(n, 2), rem(n, 2)
                h, ours = turn(m, col.same, step)
                hops = at(col.hops, m)
                live = ours & (h <= hops)
                first, second = (where(m == 0, col.need[0][k], col.need[1][k]) for k in (0, 1))
                there = at(col.hop_in, m)
                due = where((col.same == 1) & (there > 0), 2 * there - 1 + m, there)

                @pl.when(live & (h >= 1))
                def _():
                    col_copy(m, h - 1, q).wait_recv()

                @pl.when(live & (h < hops))
                def _():
                    col_copy(m, h, q).start()

                @pl.when(live & (h == at(col.hop_out, m)))
                def _():
                    x_copy(m, q).start()

                @pl.when(live & ((h == first) | (h == second)))
                def _():
                    pair_copy(m, h, col.odd + where(h == second, 2, 0), q, q).start()

                @pl.when(step == due + LAG)
                def _():
                    x_copy(m, q).wait_recv()
                    last_copy(m, q).start()

                @pl.when(step == due + 2 * LAG)
                def _():
                    last_copy(m, q).wait_recv()

                @pl.when((step == due + LAG) | (step == due + 2 * LAG))
                def _():
                    slot = where(step == due + LAG, CROSS, LAST)
                    s = where(step == due + LAG, at(col.cross_s, m), at(col.last_s, m))
                    pair_copy(m, slot, s, q, q).start()

        @pl.loop(0, WINDOW)
        def _(s):
            @pl.when((row.zero == 0) | (s != row.zero_s))
            def _():
                @pl.loop(0, 2 * LOWER)
                def _(n):
                    q, m = div(n, 2), rem(n, 2)
                    pair_copy(m, GOT + s, s, q, q).wait_recv()

        @pl.when(row.zero == 1)
        def _():
            for m in (0, 1):
                keep(m).wait()


    @pl.loop(0, WINDOW)
    def _(s):
        left = [where(core == 0, pick(row.slot[m], s), GOT + s) for m in (0, 1)]
        right = [where(core == 0, GOT + s, pick(col.slot[m], s)) for m in (0, 1)]

        @pl.loop(0, TILE // WIDTH)
        def _(n):
            span = pl.ds(pl.multiple_of(n * WIDTH, WIDTH), WIDTH)
            fp = jnp.dot(
                tiles[0, left[0], :HALF], tiles[1, right[1], :, span],
                preferred_element_type=jnp.float32,
            )
            pf = jnp.dot(
                tiles[1, left[1], :HALF], tiles[0, right[0], :, span],
                preferred_element_type=jnp.float32,
            )
            out_ref[:, span] += fp - pf

    for m in (0, 1):
        give(m).wait_send()

    @pl.loop(0, 2 * CUTS)
    def _(n):
        q, m = div(n, 2), rem(n, 2)

        @pl.when((core == 0) & (row.swap == 1))
        def _():
            swap_copy(m, q).wait_send()

        @pl.when(core == 1)
        def _():
            x_copy(m, q).wait_send()
            last_copy(m, q).wait_send()

        @pl.loop(0, HOPS)
        def _(h):
            @pl.loop(0, 2)
            def _(way):
                @pl.when((core == 0) & (h < row_hops(m, way)))
                def _():
                    row_copy(m, way, h, q).wait_send()

            @pl.when((core == 1) & (h < at(col.hops, m)))
            def _():
                col_copy(m, h, q).wait_send()

        @pl.loop(0, WINDOW)
        def _(s):
            sent = (q < LOWER) & ((row.zero == 0) | (s != row.zero_s))

            @pl.when((core == 1) | sent)
            def _():
                pair_copy(m, GOT + s, s, q, q).wait_send()


def commute(fock, density, off):
    sems = [(2, 2)] + [(2,)] * 2 + [(2, 2, HOPS, CUTS)] * 2 + [(2, CUTS)] * 2
    sems += [(2, HOPS, CUTS)] * 2 + [(2, CUTS)] * 4 + [(2, WINDOW, CUTS)] * 2
    return pl.pallas_call(
        functools.partial(kernel, off),
        out_shape=jax.ShapeDtypeStruct((HALF, TILE), jnp.float32),
        in_specs=[pl.BlockSpec(memory_space=pl.ANY)] * 2,
        out_specs=pl.BlockSpec(memory_space=pltpu.VMEM),
        scratch_shapes=[
            pltpu.VMEM((2, GOT + WINDOW, TILE, TILE), jnp.bfloat16),
        ] + [pltpu.SemaphoreType.DMA(shape) for shape in sems],
        compiler_params=pltpu.CompilerParams(
            collective_id=off, has_side_effects=True, vmem_limit_bytes=52 << 20
        ),
    )(fock, density)


def masked_piece(values, occupied, first_row, first_col):
    row_blocks = values.shape[0] // BLK
    col_blocks = values.shape[1] // BLK
    window = lax.dynamic_slice(occupied, (first_row, first_col), (row_blocks, col_blocks))
    blocks = (
        values.reshape(row_blocks, BLK, col_blocks, BLK)
        * window.astype(values.dtype)[:, None, :, None]
    )
    return blocks.reshape(values.shape)


def shards(fock_matrix, density_matrix, fock_blocks, density_blocks, slab_offset):
    corner = (lax.axis_index("row") * (HALF // BLK), lax.axis_index("col") * (TILE // BLK))
    fock = masked_piece(fock_matrix, fock_blocks, *corner)
    density = masked_piece(density_matrix, density_blocks, *corner)
    fock, density = lax.optimization_barrier((fock, density))
    branches = [functools.partial(commute, off=off) for off in range(GRID)]
    return lax.switch(slab_offset[0] % GRID, branches, fock, density)


def solution(mesh):
    placed = (P("row", "col"), P("row", "col"), P(), P(), P())
    return jax.shard_map(
        shards, mesh=mesh, in_specs=placed, out_specs=P("row", "col"), check_vma=False
    )
```

```python
import functools

import jax
import jax.numpy as jnp
import numpy as np
from jax import lax
from jax.experimental import pallas as pl
from jax.experimental.pallas import tpu as pltpu
from jax.sharding import PartitionSpec as P

BLK = 128
GRID = 16
HALF = 384
TILE = 768
WINDOW = 4
CUTS = 4
PIECE = TILE // CUTS
LOWER = CUTS // 2
HOPS = 6
LAG = 3
STEPS = HOPS + LAG
SWAPPED, OWN = 12, 13
CROSS, LAST = 7, 8
GOT = 14
WIDTH = 256
MESH = pl.DeviceIdType.MESH


def div(a, b):
    return a // b if isinstance(a, int) else lax.div(a, np.int32(b))


def rem(a, b):
    return a % b if isinstance(a, int) else lax.rem(a, np.int32(b))


def where(cond, a, b):
    if isinstance(cond, bool):
        return a if cond else b
    return jnp.where(cond, a, b)


def flag(cond):
    return where(cond, 1, 0)


def at(pair, n):
    return where(n == 0, pair[0], pair[1])


def differ(a, b):
    return a + b - 2 * a * b


class RowRoute:
    def __init__(self, i, y, off):
        t = rem(i + off, GRID)
        base = rem(t + 2, 8) - 2
        flip = rem(div(t + 2, 8), 2)
        first = (
            where(base <= 3, 4, 0),
            where(base == 0, 2, where(base == 1, 1, where(base == 4, 3, 2 * flag(base == 5)))),
        )
        self.y = y
        self.flip = (flip, where(base < 0, flip, 1 - flip))
        self.low = (where(base < 0, 0, base), where(base < 0, 1, 5 - base))
        self.swap = where(base <= 0, flip, where(base == 5, 1 - flip, 0))
        self.zero = flag((base <= 0) | (base == 5)) * (1 - self.swap)
        self.zero_s = where(base == 5, 3, where(base < 0, -base, 0))
        self.base, self.far = base, where(base < 0, 0, 8)
        self.start = tuple(
            flag(base < 0) * self.swap * self.first_turned(way) for way in (0, 1)
        )
        self.hops, self.slot = [], []
        for a in first:
            down = where(base < 0, base + 3, where(a > 0, base + a - 1, 0))
            up = where(base < 0, -base, where(a < 4, 8 - base - a, 0))
            self.hops.append((down, up))
            slots = []
            for s in range(4):
                d = base + s
                from_down = where(base < 0, flag(d >= 0), flag(s < a))
                hop = where(from_down == 1, d, where(base < 0, -d, 8 - d))
                turned = where(from_down == 1, self.flip[0], self.flip[1])
                moved = where(from_down == 1, hop - 1, hop + HOPS - 1)
                slots.append(where(hop == 0, OWN - turned, moved))
            self.slot.append(slots)
        self.both = tuple(flag(self.hops[0][w] * self.hops[1][w] > 0) for w in (0, 1))

    def step_of(self, way, h):
        return where(way == 0, h, self.far - h) - self.base

    def first_turned(self, way):
        source = self.y if way == 0 else 7 - self.y
        low = where(self.low[way] > 1, self.low[way], 1)
        return differ(self.flip[way], flag(low > source))

    def crosses(self, way, h):
        source = where(way == 0, rem(self.y + h, 8), 7 - rem(self.y + 8 - h, 8))
        low, flip = at(self.low, way), at(self.flip, way)
        now = differ(flip, flag(where(h > low, h, low) > source))
        new = differ(flip, flag(where(h + 1 > low, h + 1, low) > source))
        return differ(where(h == 0, at(self.start, way), now), new)


class ColRoute:
    def __init__(self, j, x_hi, off):
        t = rem(j + off, GRID)
        odd = rem(t, 2)
        u = rem(div(t + odd, 2), 8)
        self.down = (
            flag(u <= 3),
            where(u <= 1, 1, where(u == 4, 1, where(u == 2, odd, where(u == 5, odd, 0)))),
        )
        self.last_down = (where(u == 3, 1, where(u == 4, 0, 1 - odd)), 1 - odd)
        self.same = flag(self.down[0] == self.down[1])
        self.hops = [where(n == 1, u + 1, 8 - u) for n in self.down]
        self.need = [
            (where(n == 1, u, 8 - u), where(n == 1, u + 1, 7 - u)) for n in self.down
        ]
        self.cross_s = [3 - odd - 2 * last for last in self.last_down]
        self.last_s = [1 - odd + 2 * last for last in self.last_down]
        self.odd = odd
        self.hop_in, self.hop_out, self.slot = [], [], []
        for n, last, need in zip(self.down, self.last_down, self.need):
            w_in = u + x_hi - odd + 1 - last
            w_out = u + 1 - x_hi - odd + 1 - last
            self.hop_in.append(where(n == 1, w_in, 8 - w_in))
            self.hop_out.append(where(n == 1, w_out, 8 - w_out))
            low, high = LAST - last, CROSS + last
            self.slot.append([
                where(odd == 0, need[0], low), where(odd == 1, need[0], low),
                where(odd == 0, need[1], high), where(odd == 1, need[1], high),
            ])


def pick(values, s):
    out = values[-1]
    for n in range(len(values) - 2, -1, -1):
        out = jnp.where(s == n, values[n], out)
    return out


def kernel(
    off, fock_ref, density_ref, out_ref, tiles,
    load_sem, give_send, give_recv, row_send, row_recv, swap_send, swap_recv,
    col_send, col_recv, x_send, x_recv, last_send, last_recv, pair_send, pair_recv,
):
    r, c = lax.axis_index("row"), lax.axis_index("col")
    core, x_hi, z = rem(r, 2), rem(div(r, 2), 2), div(r, 4)
    x_lo, y = div(c, 8), rem(c, 8)
    row, col = RowRoute(div(r, 2), y, off), ColRoute(c, x_hi, off)
    y_next = (rem(y + 7, 8), rem(y + 1, 8))
    z_next = (rem(r + 28, 32), rem(r + 4, 32))
    swap_dev = (r, (1 - x_lo) * 8 + y)
    x_dev = (r + 2 - 4 * x_hi, c)
    pair_dev = (r + 1 - 2 * core, c)
    refs = (fock_ref, density_ref)
    early = (row.start[0] + row.start[1]) > 0
    late = (row.swap == 1) & ((row.start[0] + row.start[1]) == 0)

    home = where(core == 0, OWN, 0)
    away = where(core == 0, 0, OWN)
    mine = pl.ds(pl.multiple_of(core * HALF, HALF), HALF)
    other = pl.ds(pl.multiple_of(HALF - core * HALF, HALF), HALF)

    def load(m):
        return pltpu.make_async_copy(refs[m], tiles.at[m, home, mine], load_sem.at[m, 0])

    def keep(m):
        target = tiles.at[m, GOT + row.zero_s, pl.ds(0, HALF)]
        return pltpu.make_async_copy(refs[m], target, load_sem.at[m, 1])

    def remote(src, dst, send, recv, dev):
        return pltpu.make_async_remote_copy(
            src_ref=src, dst_ref=dst, send_sem=send, recv_sem=recv,
            device_id=dev, device_id_type=MESH,
        )

    def give(m):
        return remote(
            refs[m], tiles.at[m, away, mine], give_send.at[m], give_recv.at[m], pair_dev
        )

    def taken(m):
        return remote(
            refs[m], tiles.at[m, home, other], give_send.at[m], give_recv.at[m], pair_dev
        )

    for m in (0, 1):
        load(m).start()

    @pl.when((core == 1) & (row.zero == 1))
    def _():
        for m in (0, 1):
            keep(m).start()

    greet = [swap_dev, x_dev, pair_dev, (z_next[0], c), (z_next[1], c)]
    greet += [(r, x * 8 + v) for x in (0, 1) for v in y_next]
    barrier = pltpu.get_barrier_semaphore()
    for dev in greet:
        pl.semaphore_signal(barrier, inc=1, device_id=dev, device_id_type=MESH)
    pl.semaphore_wait(barrier, len(greet))

    def part(m, slot, q):
        return tiles.at[m, slot, pl.ds(pl.multiple_of(q * PIECE, PIECE), PIECE)]

    def row_copy(m, way, h, q):
        slot = where(h == 0, OWN - at(row.start, way), h - 1 + way * HOPS)
        dev = (r, differ(x_lo, row.crosses(way, h)) * 8 + at(y_next, way))
        return remote(
            part(m, slot, q), part(m, h + way * HOPS, q),
            row_send.at[m, way, h, q], row_recv.at[m, way, h, q], dev,
        )

    def row_hops(m, way):
        return where(m == 0, at(row.hops[0], way), at(row.hops[1], way))

    def swap_copy(m, q):
        return remote(
            part(m, OWN, q), part(m, SWAPPED, q),
            swap_send.at[m, q], swap_recv.at[m, q], swap_dev,
        )

    def col_copy(m, h, q):
        dev = (where(at(col.down, m) == 1, z_next[0], z_next[1]), c)
        return remote(
            part(m, h, q), part(m, h + 1, q),
            col_send.at[m, h, q], col_recv.at[m, h, q], dev,
        )

    def x_copy(m, q):
        return remote(
            part(m, at(col.hop_out, m), q), part(m, CROSS, q),
            x_send.at[m, q], x_recv.at[m, q], x_dev,
        )

    def last_copy(m, q):
        dev = (where(at(col.last_down, m) == 1, z_next[0], z_next[1]), c)
        return remote(
            part(m, CROSS, q), part(m, LAST, q),
            last_send.at[m, q], last_recv.at[m, q], dev,
        )

    def pair_copy(m, slot, s, q, to):
        return remote(
            part(m, slot, q), part(m, GOT + s, to),
            pair_send.at[m, s, to], pair_recv.at[m, s, to], pair_dev,
        )

    def turn(m, shared, step):
        odd = rem(step, 2)
        hop = where((shared == 1) & (step > 0), div(step + 1 - m, 2), step)
        ours = (shared == 0) | (step == 0) | (odd == 1 - m)
        return hop, ours

    for m in (0, 1):
        give(m).start()

    @pl.loop(0, HALF // 8)
    def _(n):
        out_ref[pl.ds(n * 8, 8)] = jnp.zeros((8, TILE), jnp.float32)

    for m in (0, 1):
        load(m).wait()

    @pl.when(core == 0)
    def _():
        @pl.loop(0, HOPS + 2)
        def _(step):
            @pl.loop(0, 4 * CUTS)
            def _(n):
                q, way, m = div(n, 4), rem(div(n, 2), 2), rem(n, 2)
                h, ours = turn(m, at(row.both, way), step)
                hops = row_hops(m, way)
                live = ours & (h <= hops)

                @pl.when((step == 0) & (n == 4 * LOWER))
                def _():
                    for k in (0, 1):
                        taken(k).wait_recv()

                @pl.when(early & (step == 0) & (way == 0))
                def _():
                    swap_copy(m, q).start()

                @pl.when(live & (h >= 1))
                def _():
                    row_copy(m, way, h - 1, q).wait_recv()

                @pl.when(live & (h < hops) & ((h >= 1) | (at(row.start, way) == 0)))
                def _():
                    row_copy(m, way, h, q).start()

                @pl.when(live & (h >= 1) & (h >= at(row.low, way)) & (q >= LOWER))
                def _():
                    slot = h - 1 + way * HOPS
                    pair_copy(m, slot, row.step_of(way, h), q, q - LOWER).start()

            @pl.when((step == 0) & (row.swap == 1))
            def _():
                @pl.loop(0, 2 * CUTS)
                def _(n):
                    q, m = div(n, 2), rem(n, 2)

                    @pl.when(late)
                    def _():
                        swap_copy(m, q).start()

                    @pl.when(early)
                    def _():
                        swap_copy(m, q).wait_recv()

                        @pl.loop(0, 2)
                        def _(way):
                            @pl.when((at(row.start, way) == 1) & (row_hops(m, way) > 0))
                            def _():
                                row_copy(m, way, 0, q).start()

            @pl.when((step == HOPS + 1) & (row.swap == 1))
            def _():
                @pl.loop(0, 2 * CUTS)
                def _(n):
                    q, m = div(n, 2), rem(n, 2)

                    @pl.when(late)
                    def _():
                        swap_copy(m, q).wait_recv()

                    @pl.when(q >= LOWER)
                    def _():
                        pair_copy(m, SWAPPED, row.zero_s, q, q - LOWER).start()

    @pl.when(core == 1)
    def _():
        @pl.loop(0, STEPS + 1)
        def _(step):
            @pl.loop(0, 2 * CUTS)
            def _(n):
                q, m = rem(div(n, 2) + LOWER, CUTS), rem(n, 2)

                @pl.when((step == 0) & (n == 2 * LOWER))
                def _():
                    for k in (0, 1):
                        taken(k).wait_recv()

                h, ours = turn(m, col.same, step)
                hops = at(col.hops, m)
                live = ours & (h <= hops)
                first, second = (where(m == 0, col.need[0][k], col.need[1][k]) for k in (0, 1))
                there = at(col.hop_in, m)
                due = where((col.same == 1) & (there > 0), 2 * there - 1 + m, there)

                @pl.when(live & (h >= 1))
                def _():
                    col_copy(m, h - 1, q).wait_recv()

                @pl.when(live & (h < hops))
                def _():
                    col_copy(m, h, q).start()

                @pl.when(live & (h == at(col.hop_out, m)))
                def _():
                    x_copy(m, q).start()

                @pl.when(live & ((h == first) | (h == second)))
                def _():
                    pair_copy(m, h, col.odd + where(h == second, 2, 0), q, q).start()

                @pl.when(step == due + LAG)
                def _():
                    x_copy(m, q).wait_recv()
                    last_copy(m, q).start()
                    pair_copy(m, CROSS, at(col.cross_s, m), q, q).start()

    order = (col.odd, col.odd + 2, col.cross_s[1], col.last_s[1])

    @pl.loop(0, WINDOW)
    def _(k):
        s = pick(order, k)

        @pl.when((core == 1) & (k == 2))
        def _():
            @pl.loop(0, 2 * CUTS)
            def _(n):
                q, m = rem(div(n, 2) + LOWER, CUTS), rem(n, 2)
                last_copy(m, q).wait_recv()
                pair_copy(m, LAST, at(col.last_s, m), q, q).start()

        kept = (core == 1) & (row.zero == 1) & (s == row.zero_s)

        @pl.when(kept)
        def _():
            for m in (0, 1):
                keep(m).wait()

        @pl.loop(0, 2 * CUTS)
        def _(n):
            q, m = div(n, 2), rem(n, 2)

            @pl.when((core == 0) | ((q < LOWER) & jnp.logical_not(kept)))
            def _():
                pair_copy(m, GOT + s, s, q, q).wait_recv()

        left = [where(core == 0, pick(row.slot[m], s), GOT + s) for m in (0, 1)]
        right = [where(core == 0, GOT + s, pick(col.slot[m], s)) for m in (0, 1)]

        @pl.loop(0, TILE // WIDTH)
        def _(n):
            span = pl.ds(pl.multiple_of(n * WIDTH, WIDTH), WIDTH)
            fp = jnp.dot(
                tiles[0, left[0], :HALF], tiles[1, right[1], :, span],
                preferred_element_type=jnp.float32,
            )
            pf = jnp.dot(
                tiles[1, left[1], :HALF], tiles[0, right[0], :, span],
                preferred_element_type=jnp.float32,
            )
            out_ref[:, span] += fp - pf

    for m in (0, 1):
        give(m).wait_send()

    @pl.loop(0, 2 * CUTS)
    def _(n):
        q, m = div(n, 2), rem(n, 2)

        @pl.when((core == 0) & (row.swap == 1))
        def _():
            swap_copy(m, q).wait_send()

        @pl.when(core == 1)
        def _():
            x_copy(m, q).wait_send()
            last_copy(m, q).wait_send()

        @pl.loop(0, HOPS)
        def _(h):
            @pl.loop(0, 2)
            def _(way):
                @pl.when((core == 0) & (h < row_hops(m, way)))
                def _():
                    row_copy(m, way, h, q).wait_send()

            @pl.when((core == 1) & (h < at(col.hops, m)))
            def _():
                col_copy(m, h, q).wait_send()

        @pl.loop(0, WINDOW)
        def _(s):
            sent = (q < LOWER) & ((row.zero == 0) | (s != row.zero_s))

            @pl.when((core == 1) | sent)
            def _():
                pair_copy(m, GOT + s, s, q, q).wait_send()


def commute(fock, density, off):
    sems = [(2, 2)] + [(2,)] * 2 + [(2, 2, HOPS, CUTS)] * 2 + [(2, CUTS)] * 2
    sems += [(2, HOPS, CUTS)] * 2 + [(2, CUTS)] * 4 + [(2, WINDOW, CUTS)] * 2
    return pl.pallas_call(
        functools.partial(kernel, off),
        out_shape=jax.ShapeDtypeStruct((HALF, TILE), jnp.float32),
        in_specs=[pl.BlockSpec(memory_space=pl.ANY)] * 2,
        out_specs=pl.BlockSpec(memory_space=pltpu.VMEM),
        scratch_shapes=[
            pltpu.VMEM((2, GOT + WINDOW, TILE, TILE), jnp.bfloat16),
        ] + [pltpu.SemaphoreType.DMA(shape) for shape in sems],
        compiler_params=pltpu.CompilerParams(
            collective_id=off, has_side_effects=True, vmem_limit_bytes=52 << 20
        ),
    )(fock, density)


def masked_piece(values, occupied, first_row, first_col):
    row_blocks = values.shape[0] // BLK
    col_blocks = values.shape[1] // BLK
    window = lax.dynamic_slice(occupied, (first_row, first_col), (row_blocks, col_blocks))
    blocks = (
        values.reshape(row_blocks, BLK, col_blocks, BLK)
        * window.astype(values.dtype)[:, None, :, None]
    )
    return blocks.reshape(values.shape)


def shards(fock_matrix, density_matrix, fock_blocks, density_blocks, slab_offset):
    corner = (lax.axis_index("row") * (HALF // BLK), lax.axis_index("col") * (TILE // BLK))
    fock = masked_piece(fock_matrix, fock_blocks, *corner)
    density = masked_piece(density_matrix, density_blocks, *corner)
    fock, density = lax.optimization_barrier((fock, density))
    branches = [functools.partial(commute, off=off) for off in range(GRID)]
    return lax.switch(slab_offset[0] % GRID, branches, fock, density)


def solution(mesh):
    placed = (P("row", "col"), P("row", "col"), P(), P(), P())
    return jax.shard_map(
        shards, mesh=mesh, in_specs=placed, out_specs=P("row", "col"), check_vma=False
    )
```

```python
import functools

import jax
import jax.numpy as jnp
import numpy as np
from jax import lax
from jax.experimental import pallas as pl
from jax.experimental.pallas import tpu as pltpu
from jax.sharding import PartitionSpec as P

BLK = 128
GRID = 16
HALF = 384
TILE = 768
WINDOW = 4
CUTS = 4
PIECE = TILE // CUTS
LOWER = CUTS // 2
HOPS = 6
LAG = 3
STEPS = HOPS + LAG
SWAPPED, OWN = 12, 13
CROSS, LAST = 7, 8
GOT = 14
WIDTH = 256
MESH = pl.DeviceIdType.MESH


def div(a, b):
    return a // b if isinstance(a, int) else lax.div(a, np.int32(b))


def rem(a, b):
    return a % b if isinstance(a, int) else lax.rem(a, np.int32(b))


def where(cond, a, b):
    if isinstance(cond, bool):
        return a if cond else b
    return jnp.where(cond, a, b)


def flag(cond):
    return where(cond, 1, 0)


def at(pair, n):
    return where(n == 0, pair[0], pair[1])


def differ(a, b):
    return a + b - 2 * a * b


class RowRoute:
    def __init__(self, i, y, off):
        t = rem(i + off, GRID)
        base = rem(t + 2, 8) - 2
        flip = rem(div(t + 2, 8), 2)
        first = (
            where(base <= 3, 4, 0),
            where(base == 0, 2, where(base == 1, 1, where(base == 4, 3, 2 * flag(base == 5)))),
        )
        self.y = y
        self.flip = (flip, where(base < 0, flip, 1 - flip))
        self.low = (where(base < 0, 0, base), where(base < 0, 1, 5 - base))
        self.swap = where(base <= 0, flip, where(base == 5, 1 - flip, 0))
        self.zero = flag((base <= 0) | (base == 5)) * (1 - self.swap)
        self.zero_s = where(base == 5, 3, where(base < 0, -base, 0))
        self.base, self.far = base, where(base < 0, 0, 8)
        self.start = tuple(
            flag(base < 0) * self.swap * self.first_turned(way) for way in (0, 1)
        )
        self.hops, self.slot = [], []
        for a in first:
            down = where(base < 0, base + 3, where(a > 0, base + a - 1, 0))
            up = where(base < 0, -base, where(a < 4, 8 - base - a, 0))
            self.hops.append((down, up))
            slots = []
            for s in range(4):
                d = base + s
                from_down = where(base < 0, flag(d >= 0), flag(s < a))
                hop = where(from_down == 1, d, where(base < 0, -d, 8 - d))
                turned = where(from_down == 1, self.flip[0], self.flip[1])
                moved = where(from_down == 1, hop - 1, hop + HOPS - 1)
                slots.append(where(hop == 0, OWN - turned, moved))
            self.slot.append(slots)
        self.both = tuple(flag(self.hops[0][w] * self.hops[1][w] > 0) for w in (0, 1))

    def step_of(self, way, h):
        return where(way == 0, h, self.far - h) - self.base

    def first_turned(self, way):
        source = self.y if way == 0 else 7 - self.y
        low = where(self.low[way] > 1, self.low[way], 1)
        return differ(self.flip[way], flag(low > source))

    def crosses(self, way, h):
        source = where(way == 0, rem(self.y + h, 8), 7 - rem(self.y + 8 - h, 8))
        low, flip = at(self.low, way), at(self.flip, way)
        now = differ(flip, flag(where(h > low, h, low) > source))
        new = differ(flip, flag(where(h + 1 > low, h + 1, low) > source))
        return differ(where(h == 0, at(self.start, way), now), new)


class ColRoute:
    def __init__(self, j, x_hi, off):
        t = rem(j + off, GRID)
        odd = rem(t, 2)
        u = rem(div(t + odd, 2), 8)
        self.down = (
            flag(u <= 3),
            where(u <= 1, 1, where(u == 4, 1, where(u == 2, odd, where(u == 5, odd, 0)))),
        )
        self.last_down = (where(u == 3, 1, where(u == 4, 0, 1 - odd)), 1 - odd)
        self.same = flag(self.down[0] == self.down[1])
        self.hops = [where(n == 1, u + 1, 8 - u) for n in self.down]
        self.need = [
            (where(n == 1, u, 8 - u), where(n == 1, u + 1, 7 - u)) for n in self.down
        ]
        self.cross_s = [3 - odd - 2 * last for last in self.last_down]
        self.last_s = [1 - odd + 2 * last for last in self.last_down]
        self.odd = odd
        self.hop_in, self.hop_out, self.slot = [], [], []
        for n, last, need in zip(self.down, self.last_down, self.need):
            w_in = u + x_hi - odd + 1 - last
            w_out = u + 1 - x_hi - odd + 1 - last
            self.hop_in.append(where(n == 1, w_in, 8 - w_in))
            self.hop_out.append(where(n == 1, w_out, 8 - w_out))
            low, high = LAST - last, CROSS + last
            self.slot.append([
                where(odd == 0, need[0], low), where(odd == 1, need[0], low),
                where(odd == 0, need[1], high), where(odd == 1, need[1], high),
            ])


def pick(values, s):
    out = values[-1]
    for n in range(len(values) - 2, -1, -1):
        out = jnp.where(s == n, values[n], out)
    return out


def kernel(
    off, fock_ref, density_ref, out_ref, tiles,
    load_sem, give_send, give_recv, row_send, row_recv, swap_send, swap_recv,
    col_send, col_recv, x_send, x_recv, last_send, last_recv, pair_send, pair_recv,
):
    r, c = lax.axis_index("row"), lax.axis_index("col")
    core, x_hi, z = rem(r, 2), rem(div(r, 2), 2), div(r, 4)
    x_lo, y = div(c, 8), rem(c, 8)
    row, col = RowRoute(div(r, 2), y, off), ColRoute(c, x_hi, off)
    y_next = (rem(y + 7, 8), rem(y + 1, 8))
    z_next = (rem(r + 28, 32), rem(r + 4, 32))
    swap_dev = (r, (1 - x_lo) * 8 + y)
    x_dev = (r + 2 - 4 * x_hi, c)
    pair_dev = (r + 1 - 2 * core, c)
    refs = (fock_ref, density_ref)
    early = (row.start[0] + row.start[1]) > 0
    late = (row.swap == 1) & ((row.start[0] + row.start[1]) == 0)

    home = where(core == 0, OWN, 0)
    away = where(core == 0, 0, OWN)
    mine = pl.ds(pl.multiple_of(core * HALF, HALF), HALF)
    other = pl.ds(pl.multiple_of(HALF - core * HALF, HALF), HALF)

    def load(m):
        return pltpu.make_async_copy(refs[m], tiles.at[m, home, mine], load_sem.at[m, 0])

    def keep(m):
        target = tiles.at[m, GOT + row.zero_s, pl.ds(0, HALF)]
        return pltpu.make_async_copy(refs[m], target, load_sem.at[m, 1])

    def remote(src, dst, send, recv, dev):
        return pltpu.make_async_remote_copy(
            src_ref=src, dst_ref=dst, send_sem=send, recv_sem=recv,
            device_id=dev, device_id_type=MESH,
        )

    def give(m):
        return remote(
            refs[m], tiles.at[m, away, mine], give_send.at[m], give_recv.at[m], pair_dev
        )

    def taken(m):
        return remote(
            refs[m], tiles.at[m, home, other], give_send.at[m], give_recv.at[m], pair_dev
        )

    for m in (0, 1):
        load(m).start()

    @pl.when((core == 1) & (row.zero == 1))
    def _():
        for m in (0, 1):
            keep(m).start()

    greet = [swap_dev, x_dev, pair_dev, (z_next[0], c), (z_next[1], c)]
    greet += [(r, x * 8 + v) for x in (0, 1) for v in y_next]
    barrier = pltpu.get_barrier_semaphore()
    for dev in greet:
        pl.semaphore_signal(barrier, inc=1, device_id=dev, device_id_type=MESH)
    pl.semaphore_wait(barrier, len(greet))

    def part(m, slot, q):
        return tiles.at[m, slot, pl.ds(pl.multiple_of(q * PIECE, PIECE), PIECE)]

    def row_copy(m, way, h, q):
        slot = where(h == 0, OWN - at(row.start, way), h - 1 + way * HOPS)
        dev = (r, differ(x_lo, row.crosses(way, h)) * 8 + at(y_next, way))
        return remote(
            part(m, slot, q), part(m, h + way * HOPS, q),
            row_send.at[m, way, h, q], row_recv.at[m, way, h, q], dev,
        )

    def row_hops(m, way):
        return where(m == 0, at(row.hops[0], way), at(row.hops[1], way))

    def swap_copy(m, q):
        return remote(
            part(m, OWN, q), part(m, SWAPPED, q),
            swap_send.at[m, q], swap_recv.at[m, q], swap_dev,
        )

    def col_copy(m, h, q):
        dev = (where(at(col.down, m) == 1, z_next[0], z_next[1]), c)
        return remote(
            part(m, h, q), part(m, h + 1, q),
            col_send.at[m, h, q], col_recv.at[m, h, q], dev,
        )

    def x_copy(m, q):
        return remote(
            part(m, at(col.hop_out, m), q), part(m, CROSS, q),
            x_send.at[m, q], x_recv.at[m, q], x_dev,
        )

    def last_copy(m, q):
        dev = (where(at(col.last_down, m) == 1, z_next[0], z_next[1]), c)
        return remote(
            part(m, CROSS, q), part(m, LAST, q),
            last_send.at[m, q], last_recv.at[m, q], dev,
        )

    def pair_copy(m, slot, s, q, to):
        return remote(
            part(m, slot, q), part(m, GOT + s, to),
            pair_send.at[m, s, to], pair_recv.at[m, s, to], pair_dev,
        )

    def turn(m, shared, step):
        odd = rem(step, 2)
        hop = where((shared == 1) & (step > 0), div(step + 1 - m, 2), step)
        ours = (shared == 0) | (step == 0) | (odd == 1 - m)
        return hop, ours

    for m in (0, 1):
        give(m).start()

    @pl.loop(0, HALF // 8)
    def _(n):
        out_ref[pl.ds(n * 8, 8)] = jnp.zeros((8, TILE), jnp.float32)

    for m in (0, 1):
        load(m).wait()

    @pl.when(core == 0)
    def _():
        @pl.loop(0, HOPS + 2)
        def _(step):
            @pl.loop(0, 4 * CUTS)
            def _(n):
                q, way, m = div(n, 4), rem(div(n, 2), 2), rem(n, 2)
                h, ours = turn(m, at(row.both, way), step)
                hops = row_hops(m, way)
                live = ours & (h <= hops)

                @pl.when((step == 0) & (n == 4 * LOWER))
                def _():
                    for k in (0, 1):
                        taken(k).wait_recv()

                @pl.when(early & (step == 0) & (way == 0))
                def _():
                    swap_copy(m, q).start()

                @pl.when(live & (h >= 1))
                def _():
                    row_copy(m, way, h - 1, q).wait_recv()

                @pl.when(live & (h < hops) & ((h >= 1) | (at(row.start, way) == 0)))
                def _():
                    row_copy(m, way, h, q).start()

                @pl.when(live & (h >= 1) & (h >= at(row.low, way)) & (q >= LOWER))
                def _():
                    slot = h - 1 + way * HOPS
                    pair_copy(m, slot, row.step_of(way, h), q, q - LOWER).start()

            @pl.when((step == where(early, 0, 2)) & (row.swap == 1))
            def _():
                @pl.loop(0, 2 * CUTS)
                def _(n):
                    q, m = div(n, 2), rem(n, 2)

                    @pl.when(late)
                    def _():
                        swap_copy(m, q).start()

                    @pl.when(early)
                    def _():
                        swap_copy(m, q).wait_recv()

                        @pl.loop(0, 2)
                        def _(way):
                            @pl.when((at(row.start, way) == 1) & (row_hops(m, way) > 0))
                            def _():
                                row_copy(m, way, 0, q).start()

            @pl.when((step == HOPS + 1) & (row.swap == 1))
            def _():
                @pl.loop(0, 2 * CUTS)
                def _(n):
                    q, m = div(n, 2), rem(n, 2)

                    @pl.when(late)
                    def _():
                        swap_copy(m, q).wait_recv()

                    @pl.when(q >= LOWER)
                    def _():
                        pair_copy(m, SWAPPED, row.zero_s, q, q - LOWER).start()

    @pl.when(core == 1)
    def _():
        @pl.loop(0, STEPS + 1)
        def _(step):
            @pl.loop(0, 2 * CUTS)
            def _(n):
                q, m = rem(div(n, 2) + LOWER, CUTS), rem(n, 2)

                @pl.when((step == 0) & (n == 2 * LOWER))
                def _():
                    for k in (0, 1):
                        taken(k).wait_recv()

                h, ours = turn(m, col.same, step)
                hops = at(col.hops, m)
                live = ours & (h <= hops)
                first, second = (where(m == 0, col.need[0][k], col.need[1][k]) for k in (0, 1))
                there = at(col.hop_in, m)
                due = where((col.same == 1) & (there > 0), 2 * there - 1 + m, there)

                @pl.when(live & (h >= 1))
                def _():
                    col_copy(m, h - 1, q).wait_recv()

                @pl.when(live & (h < hops))
                def _():
                    col_copy(m, h, q).start()

                @pl.when(live & (h == at(col.hop_out, m)))
                def _():
                    x_copy(m, q).start()

                @pl.when(live & ((h == first) | (h == second)))
                def _():
                    pair_copy(m, h, col.odd + where(h == second, 2, 0), q, q).start()

                @pl.when(step == due + LAG)
                def _():
                    x_copy(m, q).wait_recv()
                    last_copy(m, q).start()
                    pair_copy(m, CROSS, at(col.cross_s, m), q, q).start()

    order = (col.odd, col.odd + 2, col.cross_s[1], col.last_s[1])

    @pl.loop(0, WINDOW)
    def _(k):
        s = pick(order, k)

        @pl.when((core == 1) & (k == 2))
        def _():
            @pl.loop(0, 2 * CUTS)
            def _(n):
                q, m = rem(div(n, 2) + LOWER, CUTS), rem(n, 2)
                last_copy(m, q).wait_recv()
                pair_copy(m, LAST, at(col.last_s, m), q, q).start()

        kept = (core == 1) & (row.zero == 1) & (s == row.zero_s)

        @pl.when(kept)
        def _():
            for m in (0, 1):
                keep(m).wait()

        @pl.loop(0, 2 * CUTS)
        def _(n):
            q, m = div(n, 2), rem(n, 2)

            @pl.when((core == 0) | ((q < LOWER) & jnp.logical_not(kept)))
            def _():
                pair_copy(m, GOT + s, s, q, q).wait_recv()

        left = [where(core == 0, pick(row.slot[m], s), GOT + s) for m in (0, 1)]
        right = [where(core == 0, GOT + s, pick(col.slot[m], s)) for m in (0, 1)]

        @pl.loop(0, TILE // WIDTH)
        def _(n):
            span = pl.ds(pl.multiple_of(n * WIDTH, WIDTH), WIDTH)
            fp = jnp.dot(
                tiles[0, left[0], :HALF], tiles[1, right[1], :, span],
                preferred_element_type=jnp.float32,
            )
            pf = jnp.dot(
                tiles[1, left[1], :HALF], tiles[0, right[0], :, span],
                preferred_element_type=jnp.float32,
            )
            out_ref[:, span] += fp - pf

    for m in (0, 1):
        give(m).wait_send()

    @pl.loop(0, 2 * CUTS)
    def _(n):
        q, m = div(n, 2), rem(n, 2)

        @pl.when((core == 0) & (row.swap == 1))
        def _():
            swap_copy(m, q).wait_send()

        @pl.when(core == 1)
        def _():
            x_copy(m, q).wait_send()
            last_copy(m, q).wait_send()

        @pl.loop(0, HOPS)
        def _(h):
            @pl.loop(0, 2)
            def _(way):
                @pl.when((core == 0) & (h < row_hops(m, way)))
                def _():
                    row_copy(m, way, h, q).wait_send()

            @pl.when((core == 1) & (h < at(col.hops, m)))
            def _():
                col_copy(m, h, q).wait_send()

        @pl.loop(0, WINDOW)
        def _(s):
            sent = (q < LOWER) & ((row.zero == 0) | (s != row.zero_s))

            @pl.when((core == 1) | sent)
            def _():
                pair_copy(m, GOT + s, s, q, q).wait_send()


def commute(fock, density, off):
    sems = [(2, 2)] + [(2,)] * 2 + [(2, 2, HOPS, CUTS)] * 2 + [(2, CUTS)] * 2
    sems += [(2, HOPS, CUTS)] * 2 + [(2, CUTS)] * 4 + [(2, WINDOW, CUTS)] * 2
    return pl.pallas_call(
        functools.partial(kernel, off),
        out_shape=jax.ShapeDtypeStruct((HALF, TILE), jnp.float32),
        in_specs=[pl.BlockSpec(memory_space=pl.ANY)] * 2,
        out_specs=pl.BlockSpec(memory_space=pltpu.VMEM),
        scratch_shapes=[
            pltpu.VMEM((2, GOT + WINDOW, TILE, TILE), jnp.bfloat16),
        ] + [pltpu.SemaphoreType.DMA(shape) for shape in sems],
        compiler_params=pltpu.CompilerParams(
            collective_id=off, has_side_effects=True, vmem_limit_bytes=52 << 20
        ),
    )(fock, density)


def masked_piece(values, occupied, first_row, first_col):
    row_blocks = values.shape[0] // BLK
    col_blocks = values.shape[1] // BLK
    window = lax.dynamic_slice(occupied, (first_row, first_col), (row_blocks, col_blocks))
    blocks = (
        values.reshape(row_blocks, BLK, col_blocks, BLK)
        * window.astype(values.dtype)[:, None, :, None]
    )
    return blocks.reshape(values.shape)


def shards(fock_matrix, density_matrix, fock_blocks, density_blocks, slab_offset):
    corner = (lax.axis_index("row") * (HALF // BLK), lax.axis_index("col") * (TILE // BLK))
    fock = masked_piece(fock_matrix, fock_blocks, *corner)
    density = masked_piece(density_matrix, density_blocks, *corner)
    fock, density = lax.optimization_barrier((fock, density))
    branches = [functools.partial(commute, off=off) for off in range(GRID)]
    return lax.switch(slab_offset[0] % GRID, branches, fock, density)


def solution(mesh):
    placed = (P("row", "col"), P("row", "col"), P(), P(), P())
    return jax.shard_map(
        shards, mesh=mesh, in_specs=placed, out_specs=P("row", "col"), check_vma=False
    )
```
